32 devices in a mesh: dp: 4 (over z), table: 8 (over y, x, core).
Axes of the slice: x: 2, y: 2, z: 4, core: 2. Of those that a mesh axis runs over, the one named last changes fastest.
Arguments:
- queries: bfloat16 [4096, 2, 512], P(('dp', 'table')), may hold values from -6 to 6
- sub_keys: bfloat16 [2, 2, 512, 256], replicated, may hold values from -0.375 to 0.375
- values: bfloat16 [512, 512, 1024], P('table', None, 'dp'), may hold values from -0.1875 to 0.1875
- slot_first: int32 [4096, 2, 4], P(('dp', 'table')), may hold values from 0 to 511, as said below
- slot_second: int32 [4096, 2, 4], P(('dp', 'table')), may hold values from 0 to 511
- cotangent: bfloat16 [4096, 1024], P(('dp', 'table')), may hold values from -6 to 6
Outputs:
- value_update: float32 [512, 512, 1024], P('table', None, 'dp')
- key_update: float32 [2, 2, 512, 256], P(None, None, ('dp', 'table'))
- clip_factor: float32 [1], replicated
The draws below stay inside these ranges and needn't reach their ends.
Inputs may be any that keep to these rules, and one draw needn't show every extreme that they name: Within each aligned block of 128 tokens (the tokens of one device), at most 192 of its 1024 slots have slot_first in any one range [r * 64, (r + 1) * 64), and exactly 192 do in one such range.
All inputs are finite; a program needn't handle non-finite values.
Results may differ from the reference program's by a relative error of at most 0.0003.
Values may be sent and summed in bfloat16 or wider, within the bound.
A program may use at most 128 MiB of HBM per device.

```python
import math
import jax
import jax.numpy as jnp
from jax import lax

NSUB = 512
DV = 1024
DK = 512
HEADS = 2
KTOP = 4
TOK_DEV = 128
HALF_DK = 256
TOKENS = 4096
BLK = 64
CAP = 192
N_TABLE = 8


def draw_slot_first(key, part):
    slot_count = TOK_DEV * HEADS * KTOP
    block_count = TOKENS // TOK_DEV
    ranking = jax.random.permutation(jax.random.fold_in(key, 3), N_TABLE)
    choices_hot = max(1, N_TABLE // 8)

    def one_block(block_key):
        subkeys = jax.random.split(block_key, 3)
        busiest = ranking[jax.random.randint(subkeys[0], (), 0, choices_hot)]
        positions = jnp.arange(slot_count, dtype=jnp.int32)
        spread_index = (positions - CAP) % (N_TABLE - 1)
        owners = jnp.where(positions < CAP, busiest, (busiest + 1 + spread_index) % N_TABLE)
        owners = jax.random.permutation(subkeys[1], owners)
        offsets = jax.random.randint(subkeys[2], (slot_count,), 0, BLK)
        return (owners * BLK + offsets).reshape(TOK_DEV, HEADS, KTOP)
    blocks = jax.vmap(one_block)(jax.random.split(jax.random.fold_in(key, 7), block_count))
    return blocks.reshape(TOKENS, HEADS, KTOP).astype(jnp.int32)


def place_ends(values, own_key, smallest, high):
    dims = values.shape
    index_at = [jax.random.randint(jax.random.fold_in(own_key, axis), (), 0, dims[axis]) for axis in range(len(dims))]
    values = values.at[tuple(index_at)].set(smallest)
    longest = dims.index(max(dims))
    index_at[longest] = (index_at[longest] + 1) % dims[longest]
    return values.at[tuple(index_at)].set(high)


def levels(rng, dims, cuts, low, top_value):
    level = 1.0
    for position, blocks in cuts:
        draws = jax.random.uniform(jax.random.fold_in(jax.random.fold_in(rng, 6), position), (blocks,), jnp.float32, low / len(cuts), top_value / len(cuts))
        level = level * jnp.repeat(jnp.exp(draws), dims[position] // blocks).reshape((-1,) + (1,) * (len(dims) - 1 - position))
    return level


def scatter_about(rng, dims, scale, most, pieces=(), kind=jnp.bfloat16):
    array = jax.random.normal(rng, dims, jnp.float32) * scale
    if len(pieces) > 0:
        array = levels(rng, dims, pieces, -0.22, 0.18) * array
    return jnp.clip(array, min=-most, max=most).astype(kind)


def setup_inputs(seed: int = 0) -> dict:
    keys = jax.random.split(jax.random.key(seed), 7)
    return {
        "queries": scatter_about(keys[0], (TOKENS, HEADS, DK), 1.0, 6.0, ((0, 32),)),
        "sub_keys": scatter_about(keys[1], (2, HEADS, NSUB, HALF_DK), HALF_DK ** -0.5, 0.375),
        "values": scatter_about(keys[2], (NSUB, NSUB, DV), DV ** -0.5, 0.1875, ((0, 8), (2, 4))),
        "slot_first": draw_slot_first(jax.random.fold_in(keys[6], 71), 0),
        "slot_second": place_ends(jax.random.randint(keys[4], (TOKENS, HEADS, KTOP), 0, NSUB), jax.random.fold_in(keys[4], 1), 0, NSUB - 1).astype(jnp.int32),
        "cotangent": scatter_about(keys[5], (TOKENS, DV), 1.0, 6.0, ((0, 32),)),
    }


limit_ratio = 5.0

def reference(queries, sub_keys, values, slot_first, slot_second, cotangent):
    half_width = DK // 2
    table_rows = values.reshape(NSUB * NSUB, DV)
    head_ids = jnp.arange(HEADS, dtype=jnp.int32)[None, :, None]
    block_count = TOKENS // TOK_DEV
    highest = lax.Precision.HIGHEST

    def visit_block(carry, records):
        value_grad, key_grad = carry
        query_block, first_block, second_block, grad_block = records
        query_first = query_block[:, :, :half_width].astype(jnp.float32)
        query_second = query_block[:, :, half_width:].astype(jnp.float32)
        key_first = sub_keys[0][head_ids, first_block].astype(jnp.float32)
        key_second = sub_keys[1][head_ids, second_block].astype(jnp.float32)
        raw_score = jnp.einsum('thc,thkc->thk', query_first, key_first, precision=highest)
        raw_score = raw_score + jnp.einsum('thc,thkc->thk', query_second, key_second, precision=highest)
        exp_score = jnp.exp(raw_score)
        weight = exp_score / lax.optimization_barrier(jnp.sum(exp_score, axis=2, keepdims=True))
        row_index = (first_block * NSUB + second_block).astype(jnp.int32)
        grad_wide = grad_block.astype(jnp.float32)
        picked_rows = table_rows[row_index].astype(jnp.float32)
        picked = jnp.einsum('tc,thkc->thk', grad_wide, picked_rows, precision=highest)
        dscore = weight * (picked - lax.optimization_barrier(jnp.sum(weight * picked, axis=2, keepdims=True)))
        updates = weight[:, :, :, None] * grad_wide[:, None, None, :]
        value_grad = value_grad.at[row_index.reshape(-1)].add(updates.reshape(-1, DV))
        labels_first = (head_ids * NSUB + first_block).reshape(-1)
        labels_second = (head_ids * NSUB + second_block).reshape(-1)
        terms_first = (dscore[:, :, :, None] * query_first[:, :, None, :]).reshape(-1, half_width)
        terms_second = (dscore[:, :, :, None] * query_second[:, :, None, :]).reshape(-1, half_width)
        sums_first = jax.ops.segment_sum(terms_first, labels_first, num_segments=HEADS * NSUB)
        sums_second = jax.ops.segment_sum(terms_second, labels_second, num_segments=HEADS * NSUB)
        key_grad = key_grad + jnp.stack([sums_first, sums_second]).reshape(2, HEADS, NSUB, half_width)
        return ((value_grad, key_grad), None)
    records = (queries.reshape(block_count, TOK_DEV, HEADS, DK), slot_first.reshape(block_count, TOK_DEV, HEADS, KTOP), slot_second.reshape(block_count, TOK_DEV, HEADS, KTOP), cotangent.reshape(block_count, TOK_DEV, DV))
    start = (jnp.zeros((NSUB * NSUB, DV), jnp.float32), jnp.zeros((2, HEADS, NSUB, half_width), jnp.float32))
    (value_grad, key_grad), _ = lax.scan(visit_block, start, records)
    total_sq = jnp.sum(value_grad * value_grad) + jnp.sum(key_grad * key_grad)
    clip_factor = jnp.minimum(1.0, limit_ratio * math.sqrt(TOKENS) / jnp.sqrt(total_sq))
    value_update = (clip_factor * value_grad).reshape(NSUB, NSUB, DV)
    key_update = clip_factor * key_grad
    return (value_update, key_update, clip_factor.reshape(1))
```

```python
import functools
import math

import jax
import jax.numpy as jnp
from jax import lax
from jax.experimental import pallas as pl
from jax.experimental.pallas import tpu as pltpu
from jax.sharding import PartitionSpec as P

limit_ratio = 5.0
BATCH = 8
MIB = 1024 * 1024


def split3(x):
    a = lax.reduce_precision(x, 8, 7)
    b = lax.reduce_precision(x - a, 8, 7)
    c = x - a - b
    return [t.astype(jnp.bfloat16) for t in (a, b, c)]


def digits(x, count):
    out = []
    for _ in range(count):
        out.append((x % 128).astype(jnp.bfloat16))
        x = x // 128
    return out


def join(rows):
    total = rows[0]
    for power, row in enumerate(rows[1:]):
        total = total + row * float(128 ** (power + 1))
    return total


def dots_kernel(rows_ref, pos_ref, values_ref, cot_ref, out_ref, table, partial):
    step = pl.program_id(0)
    chunk, columns = values_ref.shape
    piece = min(chunk, 256)

    @pl.loop(0, chunk // piece)
    def _(i):
        at = pl.multiple_of(i * piece, piece)
        to = pl.multiple_of(step * chunk + at, piece)
        table[pl.ds(to, piece), :] = values_ref[pl.ds(at, piece), :].astype(jnp.float32)

    @pl.when(step == pl.num_programs(0) - 1)
    def _():
        count = partial.shape[0]

        @pl.loop(0, count // (2 * BATCH))
        def _(b):
            base = pl.multiple_of(b * 2 * BATCH, 2 * BATCH)
            for u in range(2 * BATCH):
                row = rows_ref[base + u]
                pos = pos_ref[base + u]
                prod = table[pl.ds(row, 1), :] * cot_ref[pl.ds(pos, 1), :]
                total = prod[:, :128]
                for c in range(128, columns, 128):
                    total = total + prod[:, c : c + 128]
                partial[pl.ds(base + u, 1), :] = total

        ones = jnp.ones((8, 128), jnp.float32)
        width = 256

        @pl.loop(0, count // width)
        def _(i):
            at = pl.multiple_of(i * width, width)
            out_ref[:, pl.ds(at, width)] = lax.dot_general(
                ones,
                partial[pl.ds(at, width), :],
                (((1,), (1,)), ((), ())),
                precision=lax.Precision.HIGHEST,
                preferred_element_type=jnp.float32,
            )


def scatter_kernel(rows_ref, pos_ref, clash_ref, weight_ref, cot_ref, out_ref, sq_ref):
    total_rows, columns = out_ref.shape
    count = rows_ref.shape[0]
    batches = count // BATCH

    @pl.loop(0, total_rows // 128)
    def _(i):
        out_ref[pl.ds(pl.multiple_of(i * 128, 128), 128), :] = jnp.zeros((128, columns), jnp.float32)

    def term(b, u):
        at = u * batches + b
        return rows_ref[at], weight_ref[at] * cot_ref[pl.ds(pos_ref[at], 1), :]

    def fast(b, acc):
        terms = [term(b, u) for u in range(BATCH)]
        old = [out_ref[pl.ds(row, 1), :] for row, _ in terms]
        new = [o + t for o, (_, t) in zip(old, terms)]
        for (row, _), n in zip(terms, new):
            out_ref[pl.ds(row, 1), :] = n
        parts = [t * (o + n) for (_, t), o, n in zip(terms, old, new)]
        while len(parts) > 1:
            parts = [x + y for x, y in zip(parts[::2], parts[1::2])]
        return acc + parts[0]

    def slow(b, acc):
        for u in range(BATCH):
            row, t = term(b, u)
            o = out_ref[pl.ds(row, 1), :]
            n = o + t
            out_ref[pl.ds(row, 1), :] = n
            acc = acc + t * (o + n)
        return acc

    def body(b, acc):
        return lax.cond(clash_ref[b] == 0, functools.partial(fast, b), functools.partial(slow, b), acc)

    sq_ref[...] = lax.fori_loop(0, batches, body, jnp.zeros((1, columns), jnp.float32))


def scale_kernel(factor_ref, grad_ref, out_ref):
    out_ref[...] = grad_ref[...] * factor_ref[0]


def key_terms(dscore, query_half, key_index, key_count):
    labels = jnp.arange(key_count, dtype=jnp.int32)
    weighted = jnp.sum(
        jnp.where(key_index[:, :, :, None] == labels, dscore[:, :, :, None], 0.0), axis=2
    )
    return jnp.einsum(
        "thi,thc->hic", weighted, query_half.astype(jnp.float32), precision=lax.Precision.HIGHEST
    )


def pick_scores(query_half, keys, key_index):
    full = jnp.einsum("thc,hic->thi", query_half, keys, preferred_element_type=jnp.float32)
    labels = jnp.arange(keys.shape[1], dtype=jnp.int32)
    return jnp.sum(jnp.where(key_index[:, :, :, None] == labels, full[:, :, None, :], 0.0), axis=3)


def local(queries, sub_keys, values, slot_first, slot_second, cotangent):
    table_size = lax.axis_size("table")
    data_size = lax.axis_size("dp")
    devices = data_size * table_size
    token_count, head_count, pick_count = slot_first.shape
    half_width = queries.shape[2] // 2
    key_count = sub_keys.shape[2]
    first_block, _, column_count = values.shape
    slot_count = token_count * head_count * pick_count
    capacity = 3 * slot_count // (2 * table_size)
    table_rows = first_block * key_count
    all_tokens = token_count * devices
    both = ("dp", "table")

    cot_columns = lax.all_to_all(cotangent, "dp", split_axis=1, concat_axis=0, tiled=True)
    cot_all = lax.all_gather(cot_columns, "table", axis=0, tiled=True)

    query_first = queries[:, :, :half_width]
    query_second = queries[:, :, half_width:]
    raw_score = pick_scores(query_first, sub_keys[0], slot_first)
    raw_score = raw_score + pick_scores(query_second, sub_keys[1], slot_second)
    exp_score = jnp.exp(raw_score)
    weight = exp_score / jnp.sum(exp_score, axis=2, keepdims=True)

    first_flat = slot_first.reshape(slot_count)
    second_flat = slot_second.reshape(slot_count)
    owner = first_flat // first_block
    local_row = first_flat % first_block * key_count + second_flat
    token_row = jnp.arange(slot_count, dtype=jnp.int32) // (head_count * pick_count)
    groups = jnp.arange(table_size, dtype=jnp.int32)
    slots = jnp.arange(slot_count, dtype=jnp.int32)
    member = (groups[:, None] == owner[None, :]).astype(jnp.bfloat16)
    earlier = (slots[:, None] < slots[None, :]).astype(jnp.bfloat16)
    ahead = jnp.dot(member, earlier, preferred_element_type=jnp.float32)
    before = jnp.sum(ahead * member.astype(jnp.float32), axis=0).astype(jnp.int32)
    target = owner * capacity + before
    place = (
        target[:, None] == jnp.arange(table_size * capacity, dtype=jnp.int32)[None, :]
    ).astype(jnp.bfloat16)
    fields = jnp.stack(
        split3(weight.reshape(slot_count))
        + digits(local_row, 3)
        + digits(token_row, 2)
        + [jnp.ones((slot_count,), jnp.bfloat16)]
    )
    placed = jnp.dot(fields, place, preferred_element_type=jnp.float32)
    filler = (jnp.arange(table_size * capacity, dtype=jnp.int32) % table_rows).astype(jnp.float32)
    send = jnp.stack(
        [
            placed[0] + placed[1] + placed[2],
            jnp.where(placed[8] > 0.5, join([placed[3], placed[4], placed[5]]), filler),
            join([placed[6], placed[7]]),
        ]
    )
    send = send.reshape(3, table_size, capacity).transpose(1, 0, 2).reshape(1, table_size, 3 * capacity)
    send = jnp.broadcast_to(send, (data_size, table_size, 3 * capacity)).reshape(devices, 3 * capacity)
    records = lax.all_to_all(send, both, split_axis=0, concat_axis=0, tiled=True)
    records = records.reshape(devices, 3, capacity)
    source = jnp.arange(devices, dtype=jnp.int32)[:, None]
    base = (source % table_size * data_size + source // table_size) * token_count
    count = devices * capacity
    weight_flat = records[:, 0].reshape(count)
    rows_flat = records[:, 1].astype(jnp.int32).reshape(count)
    pos_flat = (records[:, 2].astype(jnp.int32) + base).reshape(count)

    cot_wide = cot_all.astype(jnp.float32)
    smem = pl.BlockSpec(memory_space=pltpu.SMEM)
    chunk = min(2048, table_rows)
    dots = pl.pallas_call(
        dots_kernel,
        grid=(table_rows // chunk,),
        out_shape=jax.ShapeDtypeStruct((8, count), jnp.float32),
        in_specs=[
            smem,
            smem,
            pl.BlockSpec((chunk, column_count), lambda i: (i, 0)),
            pl.BlockSpec((all_tokens, column_count), lambda i: (0, 0), pipeline_mode=pl.Buffered(1)),
        ],
        out_specs=pl.BlockSpec((8, count), lambda i: (0, 0)),
        scratch_shapes=[
            pltpu.VMEM((table_rows, column_count), jnp.float32),
            pltpu.VMEM((count, 128), jnp.float32),
        ],
        compiler_params=pltpu.CompilerParams(vmem_limit_bytes=58 * MIB),
        name="slot_dots",
    )(rows_flat, pos_flat, values.reshape(table_rows, column_count), cot_wide)
    partial_dots = dots[0].reshape(devices, capacity)
    returned = lax.all_to_all(partial_dots, both, split_axis=0, concat_axis=0, tiled=True)
    returned = jnp.sum(returned.reshape(data_size, table_size * capacity), axis=0)
    picked = jnp.sum(
        lax.dot_general(
            jnp.stack(split3(returned)),
            place,
            (((1,), (1,)), ((), ())),
            preferred_element_type=jnp.float32,
        ),
        axis=0,
    ).reshape(token_count, head_count, pick_count)
    dscore = weight * (picked - jnp.sum(weight * picked, axis=2, keepdims=True))
    key_grad = jnp.stack(
        [
            key_terms(dscore, query_first, slot_first, key_count),
            key_terms(dscore, query_second, slot_second, key_count),
        ]
    )
    by_batch = rows_flat.reshape(BATCH, count // BATCH)
    clash = jnp.zeros((count // BATCH,), jnp.bool_)
    for u in range(BATCH):
        for v in range(u):
            clash = clash | (by_batch[u] == by_batch[v])
    clash = clash.astype(jnp.int32)
    weight_flat, key_grad = lax.optimization_barrier((weight_flat, key_grad))
    key_part = lax.psum_scatter(key_grad, both, scatter_dimension=2, tiled=True)

    value_grad, value_sq = pl.pallas_call(
        scatter_kernel,
        out_shape=(
            jax.ShapeDtypeStruct((table_rows, column_count), jnp.float32),
            jax.ShapeDtypeStruct((1, column_count), jnp.float32),
        ),
        in_specs=[smem, smem, smem, smem, pl.BlockSpec(memory_space=pltpu.VMEM)],
        out_specs=(
            pl.BlockSpec(memory_space=pltpu.VMEM),
            pl.BlockSpec(memory_space=pltpu.VMEM),
        ),
        compiler_params=pltpu.CompilerParams(vmem_limit_bytes=58 * MIB),
        cost_estimate=pl.CostEstimate(
            flops=2 * count * column_count,
            bytes_accessed=6 * 4 * table_rows * column_count,
            transcendentals=0,
        ),
        name="value_scatter",
    )(rows_flat, pos_flat, clash, weight_flat, cot_wide)

    own_sq = jnp.sum(value_sq) + jnp.sum(key_part * key_part)
    all_sq = lax.all_to_all(
        jnp.broadcast_to(own_sq, (devices, 128)), both, split_axis=0, concat_axis=0, tiled=True
    )
    total_sq = jnp.sum(all_sq[:, 0])
    clip_factor = jnp.minimum(1.0, limit_ratio * math.sqrt(all_tokens) / jnp.sqrt(total_sq))
    clip_factor = clip_factor.reshape(1)
    value_update = pl.pallas_call(
        scale_kernel,
        grid=(table_rows // chunk,),
        out_shape=jax.ShapeDtypeStruct((table_rows, column_count), jnp.float32),
        in_specs=[smem, pl.BlockSpec((chunk, column_count), lambda i: (i, 0))],
        out_specs=pl.BlockSpec((chunk, column_count), lambda i: (i, 0)),
        compiler_params=pltpu.CompilerParams(vmem_limit_bytes=32 * MIB),
        name="value_scale",
    )(clip_factor, value_grad).reshape(first_block, key_count, column_count)
    key_update = clip_factor * key_part
    return (value_update, key_update, clip_factor)


def solution(mesh):
    placed = (
        P(("dp", "table"), None, None),
        P(),
        P("table", None, "dp"),
        P(("dp", "table"), None, None),
        P(("dp", "table"), None, None),
        P(("dp", "table"), None),
    )
    return jax.shard_map(
        local,
        mesh=mesh,
        in_specs=placed,
        out_specs=(P("table", None, "dp"), P(None, None, ("dp", "table"), None), P()),
        check_vma=False,
    )
```

```python
import functools
import math

import jax
import jax.numpy as jnp
from jax import lax
from jax.experimental import pallas as pl
from jax.experimental.pallas import tpu as pltpu
from jax.sharding import PartitionSpec as P

limit_ratio = 5.0
BATCH = 8
MIB = 1024 * 1024


def split3(x):
    a = lax.reduce_precision(x, 8, 7)
    b = lax.reduce_precision(x - a, 8, 7)
    c = x - a - b
    return [t.astype(jnp.bfloat16) for t in (a, b, c)]


def digits(x, count):
    out = []
    for _ in range(count):
        out.append((x % 128).astype(jnp.bfloat16))
        x = x // 128
    return out


def join(rows):
    total = rows[0]
    for power, row in enumerate(rows[1:]):
        total = total + row * float(128 ** (power + 1))
    return total


def dots_kernel(rows_ref, pos_ref, values_ref, cot_ref, out_ref, table, partial):
    step = pl.program_id(0)
    chunk, columns = values_ref.shape
    piece = min(chunk, 256)

    @pl.loop(0, chunk // piece)
    def _(i):
        at = pl.multiple_of(i * piece, piece)
        to = pl.multiple_of(step * chunk + at, piece)
        table[pl.ds(to, piece), :] = values_ref[pl.ds(at, piece), :].astype(jnp.float32)

    @pl.when(step == pl.num_programs(0) - 1)
    def _():
        count = partial.shape[0]

        @pl.loop(0, count // (2 * BATCH))
        def _(b):
            base = pl.multiple_of(b * 2 * BATCH, 2 * BATCH)
            for u in range(2 * BATCH):
                row = rows_ref[base + u]
                pos = pos_ref[base + u]
                prod = table[pl.ds(row, 1), :] * cot_ref[pl.ds(pos, 1), :]
                total = prod[:, :128]
                for c in range(128, columns, 128):
                    total = total + prod[:, c : c + 128]
                partial[pl.ds(base + u, 1), :] = total

        ones = jnp.ones((8, 128), jnp.float32)
        width = 256

        @pl.loop(0, count // width)
        def _(i):
            at = pl.multiple_of(i * width, width)
            out_ref[:, pl.ds(at, width)] = lax.dot_general(
                ones,
                partial[pl.ds(at, width), :],
                (((1,), (1,)), ((), ())),
                precision=lax.Precision.HIGHEST,
                preferred_element_type=jnp.float32,
            )


def scatter_kernel(rows_ref, pos_ref, clash_ref, weight_ref, cot_ref, out_ref, sq_ref):
    total_rows, columns = out_ref.shape
    count = rows_ref.shape[0]
    batches = count // BATCH

    @pl.loop(0, total_rows // 128)
    def _(i):
        out_ref[pl.ds(pl.multiple_of(i * 128, 128), 128), :] = jnp.zeros((128, columns), jnp.float32)

    def term(b, u):
        at = u * batches + b
        return rows_ref[at], weight_ref[at] * cot_ref[pl.ds(pos_ref[at], 1), :]

    def fast(b, acc):
        terms = [term(b, u) for u in range(BATCH)]
        old = [out_ref[pl.ds(row, 1), :] for row, _ in terms]
        new = [o + t for o, (_, t) in zip(old, terms)]
        for (row, _), n in zip(terms, new):
            out_ref[pl.ds(row, 1), :] = n
        parts = [t * (o + n) for (_, t), o, n in zip(terms, old, new)]
        while len(parts) > 1:
            parts = [x + y for x, y in zip(parts[::2], parts[1::2])]
        return acc + parts[0]

    def slow(b, acc):
        for u in range(BATCH):
            row, t = term(b, u)
            o = out_ref[pl.ds(row, 1), :]
            n = o + t
            out_ref[pl.ds(row, 1), :] = n
            acc = acc + t * (o + n)
        return acc

    def body(b, acc):
        return lax.cond(clash_ref[b] == 0, functools.partial(fast, b), functools.partial(slow, b), acc)

    sq_ref[...] = lax.fori_loop(0, batches, body, jnp.zeros((1, columns), jnp.float32))


def scale_kernel(factor_ref, grad_ref, out_ref):
    out_ref[...] = grad_ref[...] * factor_ref[0]


def partner_of(axis, bit):
    at = lax.axis_index(axis)
    upper = (at // bit) % 2
    return upper, {axis: at + bit * (1 - 2 * upper)}


def chunk_of(slot, plan, table_size):
    chunk = 0
    for level, (axis, bit) in enumerate(plan):
        if (slot >> (len(plan) - 1 - level)) & 1:
            chunk += bit * (table_size if axis == "dp" else 1)
    return chunk


def reduce_kernel(
    plans, table_size, key_ref, value_sq_ref, out_ref, total_ref,
    held, inbox, sums, sums_in, send_sem, recv_sem, sum_send, sum_recv,
):
    levels = len(plans[0])
    chunks = 2**levels
    share = out_ref.shape[1]
    barrier = pltpu.get_barrier_semaphore()
    for axis, bit in plans[0]:
        _, where = partner_of(axis, bit)
        pl.semaphore_signal(barrier, inc=1, device_id=where, device_id_type=pl.DeviceIdType.MESH)
    for lane, plan in enumerate(plans):
        for slot in range(chunks):
            row = chunk_of(slot, plan, table_size) * share
            for q in range(out_ref.shape[0]):
                held[lane, slot, q * share : (q + 1) * share, :] = key_ref[
                    q, row : row + share, lane * 128 : (lane + 1) * 128
                ]
    pl.semaphore_wait(barrier, levels)

    offsets = [0] * len(plans)
    for level in range(levels):
        size = chunks >> (level + 1)
        copies = []
        for lane, plan in enumerate(plans):
            upper, where = partner_of(*plan[level])
            give = offsets[lane] + (1 - upper) * size
            offsets[lane] = offsets[lane] + upper * size
            copy = pltpu.make_async_remote_copy(
                src_ref=held.at[lane, pl.ds(give, size)],
                dst_ref=inbox.at[lane, pl.ds(size, size)],
                send_sem=send_sem.at[lane, level],
                recv_sem=recv_sem.at[lane, level],
                device_id=where,
                device_id_type=pl.DeviceIdType.MESH,
            )
            copy.start()
            copies.append(copy)
        for lane, copy in enumerate(copies):
            copy.wait()
            keep = offsets[lane]

            @pl.loop(0, size)
            def _(i):
                held[lane, keep + i] = held[lane, keep + i] + inbox[lane, size + i]

    own = jnp.sum(value_sq_ref[...])
    for lane in range(len(plans)):
        part = held[lane, offsets[lane]]
        own = own + jnp.sum(part * part)
        for q in range(out_ref.shape[0]):
            out_ref[q, :, lane * 128 : (lane + 1) * 128] = part[q * share : (q + 1) * share, :]
    sums[0] = jnp.full((8, 128), own, jnp.float32)
    for level in range(levels):
        _, where = partner_of(*plans[0][level])
        copy = pltpu.make_async_remote_copy(
            src_ref=sums.at[level],
            dst_ref=sums_in.at[level],
            send_sem=sum_send.at[level],
            recv_sem=sum_recv.at[level],
            device_id=where,
            device_id_type=pl.DeviceIdType.MESH,
        )
        copy.start()
        copy.wait()
        sums[level + 1] = sums[level] + sums_in[level]
    total_ref[...] = sums[levels]


def reduce_keys(key_grad, value_sq, data_size, table_size):
    chunks = data_size * table_size
    kinds, heads, key_count, width = key_grad.shape
    share = key_count // chunks
    table_bits = [2**i for i in range(table_size.bit_length() - 1)]
    data_part = [("dp", 2**i) for i in range(data_size.bit_length() - 1)]
    plans = []
    for lane in range(width // 128):
        rest = table_bits[1:] if lane % 2 == 0 else table_bits[:0:-1]
        plans.append([("table", b) for b in table_bits[:1] + rest] + data_part)
    lanes, levels = len(plans), len(plans[0])
    parts = kinds * heads
    vmem = pl.BlockSpec(memory_space=pltpu.VMEM)
    key_part, total = pl.pallas_call(
        functools.partial(reduce_kernel, plans, table_size),
        out_shape=(
            jax.ShapeDtypeStruct((parts, share, width), jnp.float32),
            jax.ShapeDtypeStruct((8, 128), jnp.float32),
        ),
        in_specs=[vmem, vmem],
        out_specs=(vmem, vmem),
        scratch_shapes=[
            pltpu.VMEM((lanes, chunks, parts * share, 128), jnp.float32),
            pltpu.VMEM((lanes, chunks, parts * share, 128), jnp.float32),
            pltpu.VMEM((levels + 1, 8, 128), jnp.float32),
            pltpu.VMEM((levels, 8, 128), jnp.float32),
            pltpu.SemaphoreType.DMA((lanes, levels)),
            pltpu.SemaphoreType.DMA((lanes, levels)),
            pltpu.SemaphoreType.DMA((levels,)),
            pltpu.SemaphoreType.DMA((levels,)),
        ],
        compiler_params=pltpu.CompilerParams(
            collective_id=0, has_side_effects=True, vmem_limit_bytes=24 * MIB
        ),
        name="key_reduce",
    )(key_grad.reshape(parts, key_count, width), value_sq)
    return key_part.reshape(kinds, heads, share, width), total[0, 0]


def key_terms(dscore, query_half, key_index, key_count):
    labels = jnp.arange(key_count, dtype=jnp.int32)
    weighted = jnp.sum(
        jnp.where(key_index[:, :, :, None] == labels, dscore[:, :, :, None], 0.0), axis=2
    )
    return jnp.einsum(
        "thi,thc->hic", weighted, query_half.astype(jnp.float32), precision=lax.Precision.HIGHEST
    )


def pick_scores(query_half, keys, key_index):
    full = jnp.einsum("thc,hic->thi", query_half, keys, preferred_element_type=jnp.float32)
    labels = jnp.arange(keys.shape[1], dtype=jnp.int32)
    return jnp.sum(jnp.where(key_index[:, :, :, None] == labels, full[:, :, None, :], 0.0), axis=3)


def local(queries, sub_keys, values, slot_first, slot_second, cotangent):
    table_size = lax.axis_size("table")
    data_size = lax.axis_size("dp")
    devices = data_size * table_size
    token_count, head_count, pick_count = slot_first.shape
    half_width = queries.shape[2] // 2
    key_count = sub_keys.shape[2]
    first_block, _, column_count = values.shape
    slot_count = token_count * head_count * pick_count
    capacity = 3 * slot_count // (2 * table_size)
    table_rows = first_block * key_count
    all_tokens = token_count * devices
    both = ("dp", "table")

    cot_columns = lax.all_to_all(cotangent, "dp", split_axis=1, concat_axis=0, tiled=True)
    cot_all = lax.all_gather(cot_columns, "table", axis=0, tiled=True)

    query_first = queries[:, :, :half_width]
    query_second = queries[:, :, half_width:]
    raw_score = pick_scores(query_first, sub_keys[0], slot_first)
    raw_score = raw_score + pick_scores(query_second, sub_keys[1], slot_second)
    exp_score = jnp.exp(raw_score)
    weight = exp_score / jnp.sum(exp_score, axis=2, keepdims=True)

    first_flat = slot_first.reshape(slot_count)
    second_flat = slot_second.reshape(slot_count)
    owner = first_flat // first_block
    local_row = first_flat % first_block * key_count + second_flat
    token_row = jnp.arange(slot_count, dtype=jnp.int32) // (head_count * pick_count)
    groups = jnp.arange(table_size, dtype=jnp.int32)
    slots = jnp.arange(slot_count, dtype=jnp.int32)
    member = (groups[:, None] == owner[None, :]).astype(jnp.bfloat16)
    earlier = (slots[:, None] < slots[None, :]).astype(jnp.bfloat16)
    ahead = jnp.dot(member, earlier, preferred_element_type=jnp.float32)
    before = jnp.sum(ahead * member.astype(jnp.float32), axis=0).astype(jnp.int32)
    target = owner * capacity + before
    place = (
        target[:, None] == jnp.arange(table_size * capacity, dtype=jnp.int32)[None, :]
    ).astype(jnp.bfloat16)
    fields = jnp.stack(
        split3(weight.reshape(slot_count))
        + digits(local_row, 3)
        + digits(token_row, 2)
        + [jnp.ones((slot_count,), jnp.bfloat16)]
    )
    placed = jnp.dot(fields, place, preferred_element_type=jnp.float32)
    filler = (jnp.arange(table_size * capacity, dtype=jnp.int32) % table_rows).astype(jnp.float32)
    send = jnp.stack(
        [
            placed[0] + placed[1] + placed[2],
            jnp.where(placed[8] > 0.5, join([placed[3], placed[4], placed[5]]), filler),
            join([placed[6], placed[7]]),
        ]
    )
    send = send.reshape(3, table_size, capacity).transpose(1, 0, 2).reshape(1, table_size, 3 * capacity)
    send = jnp.broadcast_to(send, (data_size, table_size, 3 * capacity)).reshape(devices, 3 * capacity)
    records = lax.all_to_all(send, both, split_axis=0, concat_axis=0, tiled=True)
    records = records.reshape(devices, 3, capacity)
    source = jnp.arange(devices, dtype=jnp.int32)[:, None]
    base = (source % table_size * data_size + source // table_size) * token_count
    count = devices * capacity
    weight_flat = records[:, 0].reshape(count)
    rows_flat = records[:, 1].astype(jnp.int32).reshape(count)
    pos_flat = (records[:, 2].astype(jnp.int32) + base).reshape(count)

    cot_wide = cot_all.astype(jnp.float32)
    smem = pl.BlockSpec(memory_space=pltpu.SMEM)
    chunk = min(2048, table_rows)
    dots = pl.pallas_call(
        dots_kernel,
        grid=(table_rows // chunk,),
        out_shape=jax.ShapeDtypeStruct((8, count), jnp.float32),
        in_specs=[
            smem,
            smem,
            pl.BlockSpec((chunk, column_count), lambda i: (i, 0)),
            pl.BlockSpec((all_tokens, column_count), lambda i: (0, 0), pipeline_mode=pl.Buffered(1)),
        ],
        out_specs=pl.BlockSpec((8, count), lambda i: (0, 0)),
        scratch_shapes=[
            pltpu.VMEM((table_rows, column_count), jnp.float32),
            pltpu.VMEM((count, 128), jnp.float32),
        ],
        compiler_params=pltpu.CompilerParams(vmem_limit_bytes=58 * MIB),
        name="slot_dots",
    )(rows_flat, pos_flat, values.reshape(table_rows, column_count), cot_wide)
    partial_dots = dots[0].reshape(devices, capacity)
    returned = lax.all_to_all(partial_dots, both, split_axis=0, concat_axis=0, tiled=True)
    returned = jnp.sum(returned.reshape(data_size, table_size * capacity), axis=0)
    picked = jnp.sum(
        lax.dot_general(
            jnp.stack(split3(returned)),
            place,
            (((1,), (1,)), ((), ())),
            preferred_element_type=jnp.float32,
        ),
        axis=0,
    ).reshape(token_count, head_count, pick_count)
    dscore = weight * (picked - jnp.sum(weight * picked, axis=2, keepdims=True))
    key_grad = jnp.stack(
        [
            key_terms(dscore, query_first, slot_first, key_count),
            key_terms(dscore, query_second, slot_second, key_count),
        ]
    )
    by_batch = rows_flat.reshape(BATCH, count // BATCH)
    clash = jnp.zeros((count // BATCH,), jnp.bool_)
    for u in range(BATCH):
        for v in range(u):
            clash = clash | (by_batch[u] == by_batch[v])
    clash = clash.astype(jnp.int32)
    value_grad, value_sq = pl.pallas_call(
        scatter_kernel,
        out_shape=(
            jax.ShapeDtypeStruct((table_rows, column_count), jnp.float32),
            jax.ShapeDtypeStruct((1, column_count), jnp.float32),
        ),
        in_specs=[smem, smem, smem, smem, pl.BlockSpec(memory_space=pltpu.VMEM)],
        out_specs=(
            pl.BlockSpec(memory_space=pltpu.VMEM),
            pl.BlockSpec(memory_space=pltpu.VMEM),
        ),
        compiler_params=pltpu.CompilerParams(vmem_limit_bytes=58 * MIB),
        cost_estimate=pl.CostEstimate(
            flops=2 * count * column_count,
            bytes_accessed=6 * 4 * table_rows * column_count,
            transcendentals=0,
        ),
        name="value_scatter",
    )(rows_flat, pos_flat, clash, weight_flat, cot_wide)

    key_part, total_sq = reduce_keys(key_grad, value_sq, data_size, table_size)
    clip_factor = jnp.minimum(1.0, limit_ratio * math.sqrt(all_tokens) / jnp.sqrt(total_sq))
    clip_factor = clip_factor.reshape(1)
    value_update = pl.pallas_call(
        scale_kernel,
        grid=(table_rows // chunk,),
        out_shape=jax.ShapeDtypeStruct((table_rows, column_count), jnp.float32),
        in_specs=[smem, pl.BlockSpec((chunk, column_count), lambda i: (i, 0))],
        out_specs=pl.BlockSpec((chunk, column_count), lambda i: (i, 0)),
        compiler_params=pltpu.CompilerParams(vmem_limit_bytes=32 * MIB),
        name="value_scale",
    )(clip_factor, value_grad).reshape(first_block, key_count, column_count)
    key_update = clip_factor * key_part
    return (value_update, key_update, clip_factor)


def solution(mesh):
    placed = (
        P(("dp", "table"), None, None),
        P(),
        P("table", None, "dp"),
        P(("dp", "table"), None, None),
        P(("dp", "table"), None, None),
        P(("dp", "table"), None),
    )
    return jax.shard_map(
        local,
        mesh=mesh,
        in_specs=placed,
        out_specs=(P("table", None, "dp"), P(None, None, ("dp", "table"), None), P()),
        check_vma=False,
    )
```
